256 devices in a mesh: row: 16 (over x_hi, y, core), col: 16 (over z, x_lo).
Axes of the slice: x: 4 (x_hi: 2, x_lo: 2; x = x_hi * 2 + x_lo), y: 4, z: 8, core: 2. Of those that a mesh axis runs over, the one named last changes fastest.
Arguments:
- out_grad: bfloat16 [2048, 8192], P('row', 'col'), may hold values from -6 to 6
- acts: bfloat16 [2048, 28672], P('col', 'row'), may hold values from -4 to 4
- weight: bfloat16 [28672, 8192], P('row', 'col'), may hold values from -0.03125 to 0.03125
Outputs:
- input_grad: bfloat16 [2048, 28672], P('col', 'row')
- weight_grad: float32 [28672, 8192], P('row', 'col')
The draws below stay inside these ranges and needn't reach their ends.
All inputs are finite; a program needn't handle non-finite values.
Results may differ from the reference program's by a relative error of at most 0.001.
Values may be sent and summed in bfloat16 or wider, within the bound.
A program may use at most 128 MiB of HBM per device.

```python
import math
import jax
import jax.numpy as jnp
from jax import lax

D = 8192
FF = 28672
TOKENS = 2048


def raised(result, stream_key, source, target, parts, factor):
    owner, partner = [(jnp.arange(result.shape[axis_at]) // (result.shape[axis_at] // parts)).reshape([-1 if axis == axis_at else 1 for axis in range(result.ndim)]) for axis_at in (source, target)]
    chosen = jax.random.permutation(stream_key, parts)[partner]
    strong = (owner == chosen) | (owner == (partner + parts // 2) % parts)
    return jnp.where(strong, factor * result, result)


def levels(rng, extent, pieces, least, high):
    factor_of, own = 1.0, jax.random.fold_in(rng, 6)
    for dim, shards_of in pieces:
        heights = jnp.exp(jax.random.uniform(jax.random.fold_in(own, dim), (shards_of,), jnp.float32, least / len(pieces), high / len(pieces)))
        factor_of = factor_of * jnp.repeat(heights, extent[dim] // shards_of).reshape([-1 if axis == dim else 1 for axis in range(len(extent))])
    return factor_of


def centred(own_key, shape, deviation, limit, split=(), held_as=jnp.bfloat16):
    result = deviation * jax.random.normal(own_key, shape, jnp.float32)
    if split:
        result = result * levels(own_key, shape, split, -0.22, 0.18)
    return jnp.clip(result, -limit, limit).astype(held_as)


def gaussian_with(own_key, dims, spread, most, pieces, heavy, kind=jnp.bfloat16):
    result = spread * jax.random.normal(own_key, dims, jnp.float32)
    if pieces:
        result = result * levels(own_key, dims, pieces, -0.22, 0.18)
    return jnp.clip(raised(result, jax.random.fold_in(own_key, 3), *heavy), -most, most).astype(kind)


def setup_inputs(seed: int = 0) -> dict:
    splits = jax.random.split(jax.random.key(seed), 4)
    out_grad = gaussian_with(splits[0], (TOKENS, D), 1.0, 6.0, ((0, 16), (1, 16)), (1, 0, 16, 2.0))
    acts = centred(splits[1], (TOKENS, FF), 0.5, 4.0, ((0, 16), (1, 16)))
    weight = centred(splits[2], (FF, D), FF ** -0.5, 0.03125, ((0, 16), (1, 16)))
    return {"out_grad": out_grad, "acts": acts, "weight": weight}


def reference(out_grad, acts, weight):
    input_grad = lax.dot_general(out_grad, weight, (((1,), (1,)), ((), ())), preferred_element_type=jnp.float32).astype(jnp.bfloat16)
    summed = lax.dot_general(acts, out_grad, (((0,), (0,)), ((), ())), preferred_element_type=jnp.float32)
    weight_grad = summed * (1.0 / math.sqrt(TOKENS))
    return (input_grad, weight_grad)
```

```python
import functools
import math

import jax
import jax.numpy as jnp
from jax import lax
from jax.experimental import pallas as pl
from jax.experimental.pallas import tpu as pltpu
from jax.sharding import PartitionSpec as P

MESH = pl.DeviceIdType.MESH
F32, BF16 = jnp.float32, jnp.bfloat16
NZ, NY = 8, 4
TOK = 128
NJ, FC = 7, 256
TOP = 87.0


def encode(parts, out_ref, rows):
    most = functools.reduce(jnp.maximum, [jnp.max(jnp.abs(p), axis=0, keepdims=True) for p in parts])
    scale = jnp.maximum(most * 1.01, 1e-35).astype(BF16)
    gain = (2 * TOP) / scale.astype(F32)
    for i, p in enumerate(parts):
        code = jnp.exp(jnp.abs(p) * gain - TOP)
        out_ref[pl.ds(i * rows, rows), :] = jnp.where(p < 0, -code, code).astype(BF16)
    out_ref[pl.ds(len(parts) * rows, 16), :] = jnp.broadcast_to(scale, (16, 128))


def decode(in_ref, count, rows):
    scale = in_ref[pl.ds(count * rows, 16), :].astype(F32)[:1] * (1.0 / (2 * TOP))
    parts = []
    for i in range(count):
        code = in_ref[pl.ds(i * rows, rows), :].astype(F32)
        value = (jnp.log(jnp.abs(code)) + TOP) * scale
        parts.append(jnp.where(code < 0, -value, value))
    return parts


def kernel(
    lag, scaling, g_ref, a_ref, w_ref, ig_ref, wg_ref,
    gbuf, wx, abuf, pbuf, own, h_snd, h_rcv, f_snd, f_rcv, x_snd, x_rcv,
    gx_s, gx_r, gy_s, gy_r, gs_s, gs_r, w_s, w_r, a_s, a_r, r_s, r_r, x_s, x_r, o_s,
):
    row, col = lax.axis_index("row"), lax.axis_index("col")
    xh, y, core = row // (2 * NY), (row // 2) % NY, row % 2
    z, xl = col // 2, col % 2
    hub = core == xl

    def dev(xh=xh, y=y, core=core, z=z, xl=xl):
        return {"row": (xh * NY + y) * 2 + core, "col": z * 2 + xl}

    def copy(src, dst, s_sem, r_sem, to):
        return pltpu.make_async_remote_copy(
            src_ref=src, dst_ref=dst, send_sem=s_sem, recv_sem=r_sem, device_id=to, device_id_type=MESH
        )

    ring = (dev(z=(z + 1) % NZ), dev(z=(z + NZ - 1) % NZ))
    across = dev(xl=1 - xl)
    sibling = dev(core=1 - core)
    y_peers = [dev(y=(y + d) % NY) for d in (1, 2, 3)]

    for j in range(NJ):
        abuf[j, pl.ds(z * TOK, TOK), :] = a_ref[:, j * FC : (j + 1) * FC]

    peers = [*ring, across, dev(xh=1 - xh), dev(xh=1 - xh, xl=1 - xl), sibling, *y_peers]
    barrier = pltpu.get_barrier_semaphore()
    for peer in peers:
        pl.semaphore_signal(barrier, inc=1, device_id=peer, device_id_type=MESH)
    pl.semaphore_wait(barrier, len(peers))

    def a_copy(d, s, j, arriving=False):
        back = s + 1 if arriving else s
        origin = (z + NZ - back) % NZ if d == 0 else (z + back) % NZ
        start, size = (origin * TOK + d * (TOK // 2), TOK // 2) if s == 3 else (origin * TOK, TOK)
        block = abuf.at[j, pl.ds(start, size)]
        return copy(block, block, a_s.at[d, s, j], a_r.at[d, s, j], ring[d])

    def forward(s):
        @pl.loop(0, NJ)
        def _(j):
            for d in range(2):
                if s > 0:
                    a_copy(d, s - 1, j, True).wait_recv()
                a_copy(d, s, j).start()

    forward(0)

    def g_block(xh_, y_, xl_):
        return gbuf.at[xl_, pl.ds((xh_ * NY + y_) * TOK, TOK)]

    def gx_copy(to_xh, n, src_xh, src_xl):
        block = g_block(src_xh, y, src_xl)
        return copy(g_ref, block, gx_s.at[n], gx_r.at[src_xl * 2 + src_xh], dev(xh=to_xh, xl=core))

    @pl.when(hub)
    def _():
        gx_copy(1 - xh, 0, xh, xl).start()
        gbuf[xl, pl.ds((xh * NY + y) * TOK, TOK), :] = g_ref[...]

    @pl.when(jnp.logical_not(hub))
    def _():
        gx_copy(xh, 0, xh, xl).start()
        gx_copy(1 - xh, 1, xh, xl).start()

    def w_copy(j):
        rows = pl.ds(j * FC, FC)
        return copy(w_ref.at[rows], wx.at[rows], w_s.at[j], w_r.at[j], across)

    @pl.loop(0, NJ)
    def _(j):
        w_copy(j).start()

    def gy_copy(b, n, arriving=False):
        y_ = (y + NY - (n + 1)) % NY if arriving else y
        block = g_block(b % 2, y_, b // 2)
        return copy(block, block, gy_s.at[n, b], gy_r.at[n, b], y_peers[n])

    def gs_copy(b, n):
        block = g_block(b % 2, (y + NY - n) % NY, b // 2)
        return copy(block, block, gs_s.at[n, b], gs_r.at[n, b], sibling)

    @pl.when(hub)
    def _():
        for src_xh, src_xl in ((xh, 1 - xl), (1 - xh, 1 - xl), (1 - xh, xl)):
            gx_copy(xh, 0, src_xh, src_xl).wait_recv()

        @pl.loop(0, 4)
        def _(b):
            for n in (0, 2, 1):
                gy_copy(b, n).start()
            gs_copy(b, 0).start()

    forward(1)

    @pl.when(hub)
    def _():
        for n in (0, 2, 1):

            @pl.loop(0, 4)
            def _(b):
                gy_copy(b, n, True).wait_recv()
                gs_copy(b, n + 1).start()

    forward(2)

    @pl.when(jnp.logical_not(hub))
    def _():
        for n in (0, 1, 3, 2):

            @pl.loop(0, 4)
            def _(b):
                gs_copy(b, n).wait_recv()

    forward(3)

    def rs_copy(d, s, j):
        if s == 0:
            return copy(h_snd.at[d, j], h_rcv.at[d, j], r_s.at[d, s, j], r_r.at[d, s, j], ring[d])
        return copy(f_snd.at[d, s - 1, j], f_rcv.at[d, s - 1, j], r_s.at[d, s, j], r_r.at[d, s, j], ring[d])

    def halves(j, owner):
        rows = pl.ds(owner * TOK, TOK)
        return [pbuf[j, rows, :128], pbuf[j, rows, 128:]]

    def partial(j):
        w_copy(j).wait_recv()
        rows = pl.ds(j * FC, FC)
        nt = (((1,), (1,)), ((), ()))
        pbuf[j] = lax.dot_general(gbuf[xl], w_ref[rows], nt, preferred_element_type=F32) + lax.dot_general(
            gbuf[1 - xl], wx[rows], nt, preferred_element_type=F32
        )
        far = halves(j, (z + 4) % NZ)
        for d in range(2):
            encode([far[d]], h_snd.at[d, j], TOK)
            rs_copy(d, 0, j).start()

    def pass_on(s, j):
        for d in range(2):
            rs_copy(d, s - 1, j).wait_recv()
            owner = (z + 4 - s) % NZ if d == 0 else (z + 4 + s) % NZ
            parts = halves(j, owner)
            if s == 1:
                (arrived,) = decode(h_rcv.at[d, j], 1, TOK)
                parts[d] = parts[d] + arrived
            else:
                arrived = decode(f_rcv.at[d, s - 2, j], 2, TOK)
                parts = [p + q for p, q in zip(parts, arrived)]
            encode(parts, f_snd.at[d, s - 1, j], TOK)
            rs_copy(d, s, j).start()

    def finish(j):
        parts = halves(j, z)
        for d in range(2):
            rs_copy(d, 3, j).wait_recv()
            parts = [p + q for p, q in zip(parts, decode(f_rcv.at[d, 2, j], 2, TOK))]
        for i in range(2):
            ig_ref[:, pl.ds(pl.multiple_of(j * FC + i * 128, 128), 128)] = parts[i].astype(BF16)

    def x_copy(j):
        return copy(x_snd.at[j], x_rcv.at[j], x_s.at[j], x_r.at[j], across)

    def weight_part(j):
        for d in range(2):
            a_copy(d, 3, j, True).wait_recv()
        tn = (((0,), (0,)), ((), ()))
        theirs = scaling * lax.dot_general(abuf[j], gbuf[1 - xl], tn, preferred_element_type=F32)
        encode([theirs[:, i * 128 : (i + 1) * 128] for i in range(4)], x_snd.at[j], FC)
        x_copy(j).start()
        own[j] = scaling * lax.dot_general(abuf[j], gbuf[xl], tn, preferred_element_type=F32)

    def out_copy(j):
        return pltpu.make_async_copy(own.at[j], wg_ref.at[pl.ds(j * FC, FC)], o_s.at[j])

    @pl.loop(0, NJ + 4 * lag)
    def _(i):
        def at(delay, work):
            @pl.when(jnp.logical_and(i >= delay, i < NJ + delay))
            def _():
                work(i - delay)

        at(0, partial)
        at(lag, functools.partial(pass_on, 1))
        at(0, weight_part)
        at(2 * lag, functools.partial(pass_on, 2))
        at(3 * lag, functools.partial(pass_on, 3))
        at(4 * lag, finish)

    @pl.loop(0, NJ)
    def _(j):
        x_copy(j).wait_recv()
        arrived = decode(x_rcv.at[j], 4, FC)
        for i in range(4):
            lanes = slice(i * 128, (i + 1) * 128)
            own[j, :, lanes] = own[j, :, lanes] + arrived[i]
        out_copy(j).start()

    @pl.loop(0, NJ)
    def _(j):
        w_copy(j).wait_send()
        x_copy(j).wait_send()
        for d in range(2):
            for s in range(4):
                a_copy(d, s, j).wait_send()
                rs_copy(d, s, j).wait_send()
        out_copy(j).wait()

    @pl.when(hub)
    def _():
        gx_copy(1 - xh, 0, xh, xl).wait_send()

        @pl.loop(0, 4)
        def _(b):
            for n in range(3):
                gy_copy(b, n).wait_send()
            for n in range(4):
                gs_copy(b, n).wait_send()

    @pl.when(jnp.logical_not(hub))
    def _():
        gx_copy(xh, 0, xh, xl).wait_send()
        gx_copy(1 - xh, 1, xh, xl).wait_send()


def body(out_grad, acts, weight):
    dma = pltpu.SemaphoreType.DMA
    ff, features = weight.shape
    return pl.pallas_call(
        functools.partial(kernel, 1, 1.0 / math.sqrt(TOK * 16)),
        out_shape=(jax.ShapeDtypeStruct(acts.shape, BF16), jax.ShapeDtypeStruct(weight.shape, F32)),
        in_specs=[pl.BlockSpec(memory_space=pltpu.VMEM)] * 3,
        out_specs=(pl.BlockSpec(memory_space=pltpu.VMEM), pl.BlockSpec(memory_space=pl.ANY)),
        scratch_shapes=[
            pltpu.VMEM((2, NZ * TOK, features), BF16),
            pltpu.VMEM((ff, features), BF16),
            pltpu.VMEM((NJ, NZ * TOK, FC), BF16),
            pltpu.VMEM((NJ, NZ * TOK, FC), F32),
            pltpu.VMEM((NJ, FC, features), F32),
            pltpu.VMEM((2, NJ, TOK + 16, 128), BF16),
            pltpu.VMEM((2, NJ, TOK + 16, 128), BF16),
            pltpu.VMEM((2, 3, NJ, 2 * TOK + 16, 128), BF16),
            pltpu.VMEM((2, 3, NJ, 2 * TOK + 16, 128), BF16),
            pltpu.VMEM((NJ, 4 * FC + 16, 128), BF16),
            pltpu.VMEM((NJ, 4 * FC + 16, 128), BF16),
            dma((2,)), dma((4,)),
            dma((3, 4)), dma((3, 4)),
            dma((4, 4)), dma((4, 4)),
            dma((NJ,)), dma((NJ,)),
            dma((2, 4, NJ)), dma((2, 4, NJ)),
            dma((2, 4, NJ)), dma((2, 4, NJ)),
            dma((NJ,)), dma((NJ,)),
            dma((NJ,)),
        ],
        compiler_params=pltpu.CompilerParams(
            collective_id=0, has_side_effects=True, vmem_limit_bytes=58 * 2**20
        ),
        cost_estimate=pl.CostEstimate(
            flops=8 * NZ * TOK * ff * features, bytes_accessed=16 * 2**20, transcendentals=6 * 2**20
        ),
    )(out_grad, acts, weight)


def solution(mesh):
    in_specs = (P("row", "col"), P("col", "row"), P("row", "col"))
    out_specs = (P("col", "row"), P("row", "col"))
    return jax.shard_map(body, mesh=mesh, in_specs=in_specs, out_specs=out_specs, check_vma=False)
```

```python
import functools
import math

import jax
import jax.numpy as jnp
from jax import lax
from jax.experimental import pallas as pl
from jax.experimental.pallas import tpu as pltpu
from jax.sharding import PartitionSpec as P

MESH = pl.DeviceIdType.MESH
F32, BF16 = jnp.float32, jnp.bfloat16
NZ, NY = 8, 4
TOK = 128
NJ, FC = 7, 256
TOP = 87.0


def encode(parts, out_ref, rows):
    most = functools.reduce(jnp.maximum, [jnp.max(jnp.abs(p), axis=0, keepdims=True) for p in parts])
    scale = jnp.maximum(most * 1.01, 1e-35).astype(BF16)
    gain = (2 * TOP) / scale.astype(F32)
    for i, p in enumerate(parts):
        code = jnp.exp(jnp.abs(p) * gain - TOP)
        out_ref[pl.ds(i * rows, rows), :] = jnp.where(p < 0, -code, code).astype(BF16)
    out_ref[pl.ds(len(parts) * rows, 16), :] = jnp.broadcast_to(scale, (16, 128))


def decode(in_ref, count, rows):
    scale = in_ref[pl.ds(count * rows, 16), :].astype(F32)[:1] * (1.0 / (2 * TOP))
    parts = []
    for i in range(count):
        code = in_ref[pl.ds(i * rows, rows), :].astype(F32)
        value = (jnp.log(jnp.abs(code)) + TOP) * scale
        parts.append(jnp.where(code < 0, -value, value))
    return parts


def kernel(
    lag, scaling, g_ref, a_ref, w_ref, ig_ref, wg_ref,
    gbuf, wx, w_here, abuf, pbuf, h_snd, h_rcv, f_snd, f_rcv, x_snd, x_rcv,
    gx_s, gx_r, gy_s, gy_r, gs_s, gs_r, w_s, w_r, a_s, a_r, r_s, r_r, x_s, x_r, l_s,
):
    row, col = lax.axis_index("row"), lax.axis_index("col")
    xh, y, core = row // (2 * NY), (row // 2) % NY, row % 2
    z, xl = col // 2, col % 2
    hub = core == xl

    def dev(xh=xh, y=y, core=core, z=z, xl=xl):
        return {"row": (xh * NY + y) * 2 + core, "col": z * 2 + xl}

    def copy(src, dst, s_sem, r_sem, to):
        return pltpu.make_async_remote_copy(
            src_ref=src, dst_ref=dst, send_sem=s_sem, recv_sem=r_sem, device_id=to, device_id_type=MESH
        )

    ring = (dev(z=(z + 1) % NZ), dev(z=(z + NZ - 1) % NZ))
    across = dev(xl=1 - xl)
    sibling = dev(core=1 - core)
    y_peers = [dev(y=(y + d) % NY) for d in (1, 2, 3)]

    def a_load(j):
        lanes = pl.ds(pl.multiple_of(j * FC, FC), FC)
        return pltpu.make_async_copy(a_ref.at[:, lanes], abuf.at[j, pl.ds(z * TOK, TOK)], l_s.at[j])

    w_load = pltpu.make_async_copy(w_ref, w_here, l_s.at[NJ])
    g_load = pltpu.make_async_copy(g_ref, gbuf.at[xl, pl.ds((xh * NY + y) * TOK, TOK)], l_s.at[NJ + 1])
    for j in range(NJ):
        a_load(j).start()

    @pl.when(hub)
    def _():
        g_load.start()

    w_load.start()

    peers = [*ring, across, dev(xh=1 - xh), dev(xh=1 - xh, xl=1 - xl), sibling, *y_peers]
    barrier = pltpu.get_barrier_semaphore()
    for peer in peers:
        pl.semaphore_signal(barrier, inc=1, device_id=peer, device_id_type=MESH)
    pl.semaphore_wait(barrier, len(peers))

    def a_copy(d, s, j, arriving=False):
        back = s + 1 if arriving else s
        origin = (z + NZ - back) % NZ if d == 0 else (z + back) % NZ
        start, size = (origin * TOK + d * (TOK // 2), TOK // 2) if s == 3 else (origin * TOK, TOK)
        block = abuf.at[j, pl.ds(start, size)]
        return copy(block, block, a_s.at[d, s, j], a_r.at[d, s, j], ring[d])

    def forward(s):
        @pl.loop(0, NJ)
        def _(j):
            for d in range(2):
                if s > 0:
                    a_copy(d, s - 1, j, True).wait_recv()
                elif d == 0:
                    a_load(j).wait()
                a_copy(d, s, j).start()

    def g_block(xh_, y_, xl_):
        return gbuf.at[xl_, pl.ds((xh_ * NY + y_) * TOK, TOK)]

    def gx_copy(to_xh, n, src_xh, src_xl):
        block = g_block(src_xh, y, src_xl)
        return copy(g_ref, block, gx_s.at[n], gx_r.at[src_xl * 2 + src_xh], dev(xh=to_xh, xl=core))

    @pl.when(hub)
    def _():
        gx_copy(1 - xh, 0, xh, xl).start()
        g_load.wait()

    @pl.when(jnp.logical_not(hub))
    def _():
        gx_copy(xh, 0, xh, xl).start()
        gx_copy(1 - xh, 1, xh, xl).start()

    def w_copy(j):
        rows = pl.ds(j * FC, FC)
        return copy(w_ref.at[rows], wx.at[rows], w_s.at[j], w_r.at[j], across)

    @pl.loop(0, NJ)
    def _(j):
        w_copy(j).start()

    forward(0)

    def gy_copy(b, n, arriving=False):
        y_ = (y + NY - (n + 1)) % NY if arriving else y
        block = g_block(b % 2, y_, b // 2)
        return copy(block, block, gy_s.at[n, b], gy_r.at[n, b], y_peers[n])

    def gs_copy(b, n):
        block = g_block(b % 2, (y + NY - n) % NY, b // 2)
        return copy(block, block, gs_s.at[n, b], gs_r.at[n, b], sibling)

    @pl.when(hub)
    def _():
        for src_xh, src_xl in ((xh, 1 - xl), (1 - xh, 1 - xl), (1 - xh, xl)):
            gx_copy(xh, 0, src_xh, src_xl).wait_recv()

        @pl.loop(0, 4)
        def _(b):
            for n in (0, 2, 1):
                gy_copy(b, n).start()
            gs_copy(b, 0).start()

    forward(1)

    @pl.when(hub)
    def _():
        for n in (0, 2, 1):

            @pl.loop(0, 4)
            def _(b):
                gy_copy(b, n, True).wait_recv()
                gs_copy(b, n + 1).start()

    forward(2)

    @pl.when(jnp.logical_not(hub))
    def _():
        for n in (0, 1, 3, 2):

            @pl.loop(0, 4)
            def _(b):
                gs_copy(b, n).wait_recv()

    forward(3)
    w_load.wait()

    def rs_copy(d, s, j):
        if s == 0:
            return copy(h_snd.at[d, j], h_rcv.at[d, j], r_s.at[d, s, j], r_r.at[d, s, j], ring[d])
        return copy(f_snd.at[d, s - 1, j], f_rcv.at[d, s - 1, j], r_s.at[d, s, j], r_r.at[d, s, j], ring[d])

    def halves(j, owner):
        rows = pl.ds(owner * TOK, TOK)
        return [pbuf[j, rows, :128], pbuf[j, rows, 128:]]

    def partial(j):
        w_copy(j).wait_recv()
        rows = pl.ds(j * FC, FC)
        nt = (((1,), (1,)), ((), ()))
        pbuf[j] = lax.dot_general(gbuf[xl], w_here[rows], nt, preferred_element_type=F32) + lax.dot_general(
            gbuf[1 - xl], wx[rows], nt, preferred_element_type=F32
        )
        far = halves(j, (z + 4) % NZ)
        for d in range(2):
            encode([far[d]], h_snd.at[d, j], TOK)
            rs_copy(d, 0, j).start()

    def pass_on(s, j):
        for d in range(2):
            rs_copy(d, s - 1, j).wait_recv()
            owner = (z + 4 - s) % NZ if d == 0 else (z + 4 + s) % NZ
            parts = halves(j, owner)
            if s == 1:
                (arrived,) = decode(h_rcv.at[d, j], 1, TOK)
                parts[d] = parts[d] + arrived
            else:
                arrived = decode(f_rcv.at[d, s - 2, j], 2, TOK)
                parts = [p + q for p, q in zip(parts, arrived)]
            encode(parts, f_snd.at[d, s - 1, j], TOK)
            rs_copy(d, s, j).start()

    def finish(j):
        parts = halves(j, z)
        for d in range(2):
            rs_copy(d, 3, j).wait_recv()
            parts = [p + q for p, q in zip(parts, decode(f_rcv.at[d, 2, j], 2, TOK))]
        for i in range(2):
            ig_ref[:, pl.ds(pl.multiple_of(j * FC + i * 128, 128), 128)] = parts[i].astype(BF16)

    def x_copy(j):
        return copy(x_snd.at[j], x_rcv.at[j], x_s.at[j], x_r.at[j], across)

    def weight_part(j):
        for d in range(2):
            a_copy(d, 3, j, True).wait_recv()
        tn = (((0,), (0,)), ((), ()))
        theirs = scaling * lax.dot_general(abuf[j], gbuf[1 - xl], tn, preferred_element_type=F32)
        encode([theirs[:, i * 128 : (i + 1) * 128] for i in range(4)], x_snd.at[j], FC)
        x_copy(j).start()
        wg_ref[pl.ds(j * FC, FC), :] = scaling * lax.dot_general(abuf[j], gbuf[xl], tn, preferred_element_type=F32)

    @pl.loop(0, NJ + 4 * lag)
    def _(i):
        def at(delay, work):
            @pl.when(jnp.logical_and(i >= delay, i < NJ + delay))
            def _():
                work(i - delay)

        at(0, partial)
        at(lag, functools.partial(pass_on, 1))
        at(0, weight_part)
        at(2 * lag, functools.partial(pass_on, 2))
        at(3 * lag, functools.partial(pass_on, 3))
        at(4 * lag, finish)

    @pl.loop(0, NJ)
    def _(j):
        x_copy(j).wait_recv()
        arrived = decode(x_rcv.at[j], 4, FC)
        for i in range(4):
            lanes = slice(i * 128, (i + 1) * 128)
            rows = pl.ds(j * FC, FC)
            wg_ref[rows, lanes] = wg_ref[rows, lanes] + arrived[i]

    @pl.loop(0, NJ)
    def _(j):
        w_copy(j).wait_send()
        x_copy(j).wait_send()
        for d in range(2):
            for s in range(4):
                a_copy(d, s, j).wait_send()
                rs_copy(d, s, j).wait_send()

    @pl.when(hub)
    def _():
        gx_copy(1 - xh, 0, xh, xl).wait_send()

        @pl.loop(0, 4)
        def _(b):
            for n in range(3):
                gy_copy(b, n).wait_send()
            for n in range(4):
                gs_copy(b, n).wait_send()

    @pl.when(jnp.logical_not(hub))
    def _():
        gx_copy(xh, 0, xh, xl).wait_send()
        gx_copy(1 - xh, 1, xh, xl).wait_send()


def body(out_grad, acts, weight):
    dma = pltpu.SemaphoreType.DMA
    ff, features = weight.shape
    return pl.pallas_call(
        functools.partial(kernel, 1, 1.0 / math.sqrt(TOK * 16)),
        out_shape=(pltpu.VMEM(acts.shape, BF16), pltpu.VMEM(weight.shape, F32)),
        in_specs=[pl.BlockSpec(memory_space=pltpu.HBM)] * 3,
        out_specs=(pl.BlockSpec(memory_space=pltpu.VMEM), pl.BlockSpec(memory_space=pltpu.VMEM)),
        scratch_shapes=[
            pltpu.VMEM((2, NZ * TOK, features), BF16),
            pltpu.VMEM((ff, features), BF16),
            pltpu.VMEM((ff, features), BF16),
            pltpu.VMEM((NJ, NZ * TOK, FC), BF16),
            pltpu.VMEM((NJ, NZ * TOK, FC), F32),
            pltpu.VMEM((2, NJ, TOK + 16, 128), BF16),
            pltpu.VMEM((2, NJ, TOK + 16, 128), BF16),
            pltpu.VMEM((2, 3, NJ, 2 * TOK + 16, 128), BF16),
            pltpu.VMEM((2, 3, NJ, 2 * TOK + 16, 128), BF16),
            pltpu.VMEM((NJ, 4 * FC + 16, 128), BF16),
            pltpu.VMEM((NJ, 4 * FC + 16, 128), BF16),
            dma((2,)), dma((4,)),
            dma((3, 4)), dma((3, 4)),
            dma((4, 4)), dma((4, 4)),
            dma((NJ,)), dma((NJ,)),
            dma((2, 4, NJ)), dma((2, 4, NJ)),
            dma((2, 4, NJ)), dma((2, 4, NJ)),
            dma((NJ,)), dma((NJ,)),
            dma((NJ + 2,)),
        ],
        compiler_params=pltpu.CompilerParams(
            collective_id=0, has_side_effects=True, vmem_limit_bytes=56 * 2**20
        ),
        cost_estimate=pl.CostEstimate(
            flops=8 * NZ * TOK * ff * features, bytes_accessed=16 * 2**20, transcendentals=6 * 2**20
        ),
    )(out_grad, acts, weight)


def solution(mesh):
    in_specs = (P("row", "col"), P("col", "row"), P("row", "col"))
    out_specs = (P("col", "row"), P("row", "col"))
    return jax.shard_map(body, mesh=mesh, in_specs=in_specs, out_specs=out_specs, check_vma=False)
```

```python
import functools
import math

import jax
import jax.numpy as jnp
from jax import lax
from jax.experimental import pallas as pl
from jax.experimental.pallas import tpu as pltpu
from jax.sharding import PartitionSpec as P

MESH = pl.DeviceIdType.MESH
F32, BF16 = jnp.float32, jnp.bfloat16
NZ, NY = 8, 4
TOK = 128
NJ, FC = 7, 256
HC = FC // 2
TOP = 87.0


def encode(parts, out_ref, rows):
    most = functools.reduce(jnp.maximum, [jnp.max(jnp.abs(p), axis=0, keepdims=True) for p in parts])
    scale = jnp.maximum(most * 1.01, 1e-35).astype(BF16)
    gain = (2 * TOP) / scale.astype(F32)
    for i, p in enumerate(parts):
        code = jnp.exp(jnp.abs(p) * gain - TOP)
        out_ref[pl.ds(i * rows, rows), :] = jnp.where(p < 0, -code, code).astype(BF16)
    out_ref[pl.ds(len(parts) * rows, 16), :] = jnp.broadcast_to(scale, (16, 128))


def decode(in_ref, count, rows):
    scale = in_ref[pl.ds(count * rows, 16), :].astype(F32)[:1] * (1.0 / (2 * TOP))
    parts = []
    for i in range(count):
        code = in_ref[pl.ds(i * rows, rows), :].astype(F32)
        value = (jnp.log(jnp.abs(code)) + TOP) * scale
        parts.append(jnp.where(code < 0, -value, value))
    return parts


def kernel(
    lag, scaling, g_ref, a_ref, w_ref, ig_ref, wg_ref,
    gbuf, wx, w_here, abuf, pbuf, h_snd, h_rcv, f_snd, f_rcv, x_snd, x_rcv, i_snd, i_rcv,
    gx_s, gx_r, gy_s, gy_r, gf_s, gf_r, gs_s, gs_r, w_s, w_r, a_s, a_r, r_s, r_r, x_s, x_r, i_s, i_r, l_s,
):
    row, col = lax.axis_index("row"), lax.axis_index("col")
    xh, y, core = row // (2 * NY), (row // 2) % NY, row % 2
    z, xl = col // 2, col % 2
    half = NJ * HC

    def dev(xh=xh, y=y, core=core, z=z, xl=xl):
        return {"row": (xh * NY + y) * 2 + core, "col": z * 2 + xl}

    def copy(src, dst, s_sem, r_sem, to):
        return pltpu.make_async_remote_copy(
            src_ref=src, dst_ref=dst, send_sem=s_sem, recv_sem=r_sem, device_id=to, device_id_type=MESH
        )

    ring = (dev(z=(z + 1) % NZ), dev(z=(z + NZ - 1) % NZ))
    across = dev(xl=1 - xl)
    sibling = dev(core=1 - core)
    y_peers = [dev(y=(y + d) % NY) for d in (1, 3, 2)]
    x_peers = [dev(xl=1 - xl), dev(xh=1 - xh, xl=1 - xl), dev(xh=1 - xh)]

    def a_load(j):
        lanes = pl.ds(pl.multiple_of(j * FC, FC), FC)
        return pltpu.make_async_copy(a_ref.at[:, lanes], abuf.at[j, pl.ds(z * TOK, TOK)], l_s.at[j])

    w_load = pltpu.make_async_copy(w_ref, w_here, l_s.at[NJ])
    g_load = pltpu.make_async_copy(
        g_ref, gbuf.at[xl, pl.ds(((core * 2 + xh) * NY + y) * TOK, TOK)], l_s.at[NJ + 1]
    )
    for j in range(NJ):
        a_load(j).start()

    g_load.start()
    w_load.start()

    peers = [*ring, *x_peers, sibling, *y_peers]
    barrier = pltpu.get_barrier_semaphore()
    for peer in peers:
        pl.semaphore_signal(barrier, inc=1, device_id=peer, device_id_type=MESH)
    pl.semaphore_wait(barrier, len(peers))

    def a_copy(d, s, j, arriving=False):
        back = s + 1 if arriving else s
        origin = (z + NZ - back) % NZ if d == 0 else (z + back) % NZ
        start, size = (origin * TOK + d * (TOK // 2), TOK // 2) if s == 3 else (origin * TOK, TOK)
        block = abuf.at[j, pl.ds(start, size)]
        return copy(block, block, a_s.at[d, s, j], a_r.at[d, s, j], ring[d])

    def a_step(s, j):
        if s == 0:
            a_load(j).wait()
        for d in range(2):
            if s > 0:
                a_copy(d, s - 1, j, True).wait_recv()
            a_copy(d, s, j).start()

    def slot(t):
        for s in range(4):
            if 0 <= t - s < NJ:
                a_step(s, t - s)

    def g_block(xh_, y_, xl_, core_):
        return gbuf.at[xl_, pl.ds(((core_ * 2 + xh_) * NY + y_) * TOK, TOK)]

    sources = [(xh, xl), (xh, 1 - xl), (1 - xh, 1 - xl), (1 - xh, xl)]

    def gx_copy(n, arriving=False):
        if arriving:
            src_xh, src_xl = sources[n + 1]
        else:
            src_xh, src_xl = xh, xl
        return copy(g_ref, g_block(src_xh, y, src_xl, core), gx_s.at[n], gx_r.at[n], x_peers[n])

    for n in (2, 1, 0):
        gx_copy(n).start()

    def w_copy(j):
        rows = pl.ds((1 - xl) * half + j * HC, HC)
        return copy(w_ref.at[rows], wx.at[pl.ds(j * HC, HC)], w_s.at[j], w_r.at[j], across)

    @pl.loop(0, NJ)
    def _(j):
        w_copy(j).start()

    def source(b, y_):
        return sources[b][0], y_, sources[b][1]

    def gy_copy(b, d, arriving=False):
        y_ = ((y + NY - 1) if d == 0 else (y + 1)) % NY if arriving else y
        block = g_block(*source(b, y_), core)
        return copy(block, block, gy_s.at[d, b], gy_r.at[d, b], y_peers[d])

    def gf_copy(b, arriving=False):
        d = b % 2
        y_ = (y + 2) % NY if arriving else ((y + NY - 1) if d == 0 else (y + 1)) % NY
        block = g_block(*source(b, y_), core)
        return copy(block, block, gf_s.at[b], gf_r.at[b], y_peers[d])

    def gs_copy(b, n, arriving=False):
        block = g_block(*source(b, (y + NY - n) % NY), 1 - core if arriving else core)
        return copy(block, block, gs_s.at[n, b], gs_r.at[n, b], sibling)

    def along_y(b):
        for d in range(2):
            gy_copy(b, d).start()
        gs_copy(b, 0).start()

    def further(b):
        for d in range(2):
            gy_copy(b, d, True).wait_recv()
        gf_copy(b).start()
        gs_copy(b, 1).start()
        gs_copy(b, 3).start()

    g_load.wait()
    along_y(0)
    slot(0)
    slot(1)
    for n in (0, 1):
        gx_copy(n, True).wait_recv()
        along_y(n + 1)
    slot(2)
    gx_copy(2, True).wait_recv()
    along_y(3)
    slot(3)
    further(0)
    further(1)
    slot(4)
    further(2)
    further(3)
    slot(5)
    for b in range(4):
        gf_copy(b, True).wait_recv()
        gs_copy(b, 2).start()
    w_load.wait()
    for n in (0, 1, 3, 2):
        for b in range(4):
            gs_copy(b, n, True).wait_recv()
    slot(6)

    def rs_copy(d, s, j):
        if s == 0:
            return copy(h_snd.at[d, j], h_rcv.at[d, j], r_s.at[d, s, j], r_r.at[d, s, j], ring[d])
        return copy(f_snd.at[d, s - 1, j], f_rcv.at[d, s - 1, j], r_s.at[d, s, j], r_r.at[d, s, j], ring[d])

    def halves(j, owner):
        return [pbuf[j, pl.ds((k * NZ + owner) * TOK, TOK), :] for k in range(2)]

    def partial(j):
        w_copy(j).wait_recv()
        rows = pl.ds(j * HC, HC)
        nt = (((1,), (1,)), ((), ()))
        pbuf[j] = lax.dot_general(gbuf[xl], w_here[pl.ds(xl * half + j * HC, HC)], nt, preferred_element_type=F32) + lax.dot_general(
            gbuf[1 - xl], wx[rows], nt, preferred_element_type=F32
        )
        far = halves(j, (z + 4) % NZ)
        for d in range(2):
            encode([far[d]], h_snd.at[d, j], TOK)
            rs_copy(d, 0, j).start()

    def pass_on(s, j):
        for d in range(2):
            rs_copy(d, s - 1, j).wait_recv()
            owner = (z + 4 - s) % NZ if d == 0 else (z + 4 + s) % NZ
            parts = halves(j, owner)
            if s == 1:
                (arrived,) = decode(h_rcv.at[d, j], 1, TOK)
                parts[d] = parts[d] + arrived
            else:
                arrived = decode(f_rcv.at[d, s - 2, j], 2, TOK)
                parts = [p + q for p, q in zip(parts, arrived)]
            encode(parts, f_snd.at[d, s - 1, j], TOK)
            rs_copy(d, s, j).start()

    def i_copy(j):
        return copy(i_snd.at[j], i_rcv.at[j], i_s.at[j], i_r.at[j], across)

    def finish(j):
        parts = halves(j, z)
        for d in range(2):
            rs_copy(d, 3, j).wait_recv()
            parts = [p + q for p, q in zip(parts, decode(f_rcv.at[d, 2, j], 2, TOK))]
        mine, theirs = jnp.where(xl == 0, parts[0], parts[1]), jnp.where(xl == 0, parts[1], parts[0])
        ig_ref[:, pl.ds(pl.multiple_of(xl * half + j * HC, HC), HC)] = mine.astype(BF16)
        i_snd[j] = theirs.astype(BF16)
        i_copy(j).start()

    def x_copy(j):
        return copy(x_snd.at[j], x_rcv.at[j], x_s.at[j], x_r.at[j], across)

    def weight_part(j):
        for d in range(2):
            a_copy(d, 3, j, True).wait_recv()
        tn = (((0,), (0,)), ((), ()))
        tokens = pl.ds(xl * NZ * TOK, NZ * TOK)
        theirs = scaling * lax.dot_general(abuf[j], gbuf[1 - xl, tokens], tn, preferred_element_type=F32)
        encode([theirs[:, i * 128 : (i + 1) * 128] for i in range(4)], x_snd.at[j], FC)
        x_copy(j).start()
        wg_ref[pl.ds(j * FC, FC), :] = scaling * lax.dot_general(abuf[j], gbuf[xl, tokens], tn, preferred_element_type=F32)

    @pl.loop(0, NJ + 7)
    def _(i):
        def at(delay, work):
            @pl.when(jnp.logical_and(i >= delay, i < NJ + delay))
            def _():
                work(i - delay)

        at(0, partial)
        at(1, functools.partial(pass_on, 1))
        at(0, weight_part)
        for s in (1, 2, 3):

            @pl.when(i < s)
            def _():
                a_step(s, i + NJ - s)

        at(3, functools.partial(pass_on, 2))
        at(5, functools.partial(pass_on, 3))
        at(7, finish)

    @pl.loop(0, NJ)
    def _(j):
        i_copy(j).wait_recv()
        ig_ref[:, pl.ds(pl.multiple_of((1 - xl) * half + j * HC, HC), HC)] = i_rcv[j]
        x_copy(j).wait_recv()
        arrived = decode(x_rcv.at[j], 4, FC)
        for i in range(4):
            lanes = slice(i * 128, (i + 1) * 128)
            rows = pl.ds(j * FC, FC)
            wg_ref[rows, lanes] = wg_ref[rows, lanes] + arrived[i]

    @pl.loop(0, NJ)
    def _(j):
        w_copy(j).wait_send()
        x_copy(j).wait_send()
        i_copy(j).wait_send()
        for d in range(2):
            for s in range(4):
                a_copy(d, s, j).wait_send()
                rs_copy(d, s, j).wait_send()

    for n in range(3):
        gx_copy(n).wait_send()
    for b in range(4):
        for d in range(2):
            gy_copy(b, d).wait_send()
        gf_copy(b).wait_send()
        for n in range(4):
            gs_copy(b, n).wait_send()


def body(out_grad, acts, weight):
    dma = pltpu.SemaphoreType.DMA
    ff, features = weight.shape
    return pl.pallas_call(
        functools.partial(kernel, 1, 1.0 / math.sqrt(TOK * 16)),
        out_shape=(pltpu.VMEM(acts.shape, BF16), pltpu.VMEM(weight.shape, F32)),
        in_specs=[pl.BlockSpec(memory_space=pltpu.HBM)] * 3,
        out_specs=(pl.BlockSpec(memory_space=pltpu.VMEM), pl.BlockSpec(memory_space=pltpu.VMEM)),
        scratch_shapes=[
            pltpu.VMEM((2, 2 * NZ * TOK, features), BF16),
            pltpu.VMEM((ff // 2, features), BF16),
            pltpu.VMEM((ff, features), BF16),
            pltpu.VMEM((NJ, NZ * TOK, FC), BF16),
            pltpu.VMEM((NJ, 2 * NZ * TOK, HC), F32),
            pltpu.VMEM((2, NJ, TOK + 16, 128), BF16),
            pltpu.VMEM((2, NJ, TOK + 16, 128), BF16),
            pltpu.VMEM((2, 3, NJ, 2 * TOK + 16, 128), BF16),
            pltpu.VMEM((2, 3, NJ, 2 * TOK + 16, 128), BF16),
            pltpu.VMEM((NJ, 4 * FC + 16, 128), BF16),
            pltpu.VMEM((NJ, 4 * FC + 16, 128), BF16),
            pltpu.VMEM((NJ, TOK, HC), BF16),
            pltpu.VMEM((NJ, TOK, HC), BF16),
            dma((3,)), dma((3,)),
            dma((2, 4)), dma((2, 4)),
            dma((4,)), dma((4,)),
            dma((4, 4)), dma((4, 4)),
            dma((NJ,)), dma((NJ,)),
            dma((2, 4, NJ)), dma((2, 4, NJ)),
            dma((2, 4, NJ)), dma((2, 4, NJ)),
            dma((NJ,)), dma((NJ,)),
            dma((NJ,)), dma((NJ,)),
            dma((NJ + 2,)),
        ],
        compiler_params=pltpu.CompilerParams(
            collective_id=0, has_side_effects=True, vmem_limit_bytes=56 * 2**20
        ),
        cost_estimate=pl.CostEstimate(
            flops=8 * NZ * TOK * ff * features, bytes_accessed=16 * 2**20, transcendentals=6 * 2**20
        ),
    )(out_grad, acts, weight)


def solution(mesh):
    in_specs = (P("row", "col"), P("col", "row"), P("row", "col"))
    out_specs = (P("col", "row"), P("row", "col"))
    return jax.shard_map(body, mesh=mesh, in_specs=in_specs, out_specs=out_specs, check_vma=False)
```
